256 devices in a mesh: dp: 8 (over y, core), ctx: 32 (over z, x).
Axes of the slice: x: 4, y: 4, z: 8, core: 2. Of those that a mesh axis runs over, the one named last changes fastest.
Arguments:
- events: bfloat16 [8, 8192, 512], P('dp', 'ctx'), may hold values from -6 to 6
- lengths: int32 [8, 4], P('dp'), may hold values from 1 to 16, 32 in all within a row
- block_slots: int32 [8, 32], P('dp'), may hold values from 0 to 31, each once within a row
- w_in: bfloat16 [512, 2048], P(None, 'dp'), may hold values from -64 to 64
- w_out: bfloat16 [512, 512], replicated, may hold values from -0.25 to 0.25
- w_pool: bfloat16 [512, 1024], P(None, 'dp'), may hold values from -0.25 to 0.25
- queries: bfloat16 [8, 512], replicated, may hold values from -4 to 4
Outputs:
- layer_out: bfloat16 [8, 8192, 512], P('dp', 'ctx')
- interests: float32 [8, 4, 8, 512], P('dp')
The draws below stay inside these ranges and needn't reach their ends.
Inputs may be any that keep to these rules, and one draw needn't show every extreme that they name: The lengths of a group sum to 32; the largest is exactly 16. `block_slots`: each group's row names every block once.
All inputs are finite; a program needn't handle non-finite values.
Results may differ from the reference program's by a relative error of at most 0.02.
Values may be sent and summed in bfloat16 or wider, within the bound.
No kernel may reach another device: no remote copies, remote signals or barrier semaphores. Data moves between devices by JAX's collectives and lax.ppermute only.
A program may use at most 128 MiB of HBM per device.

```python
import math
import jax
import jax.numpy as jnp
import numpy as np
from jax import lax

D = 512
H = 4
HEAD_DIMENSION = 128
NQ = 8
BLOCK = 256
USERS = 4
NBLK = 32
SEQ = 8192
MAXB = 16
N_DP = 8


def column_scales(scale_update, scale_value, scale_query, scale_key):
    column = jnp.arange(4 * D, dtype=jnp.int32)
    section = column // D
    scale_table = jnp.array([scale_update, scale_value, scale_query, scale_key], jnp.float32)
    picked = jnp.sum(jnp.where(section[:, None] == jnp.arange(4, dtype=jnp.int32)[None, :], scale_table[None, :], 0.0), axis=1)
    return picked / jnp.sqrt(jnp.float32(D))


def draw_w_in(key, part):
    key = jax.random.fold_in(key, 11)
    entries = jax.random.truncated_normal(key, -4.0, 4.0, (D, 4 * D), jnp.float32)
    scales = column_scales(3.0, 1.0, 96.0, 0.06)
    return (entries * scales[None, :]).astype(jnp.bfloat16)


def level_of(stream_key, dims, shards, least, top_value):
    gain, own = 1.0, jax.random.fold_in(stream_key, 6)
    for axis_at, blocks in shards:
        heights = jnp.exp(jax.random.uniform(jax.random.fold_in(own, axis_at), (blocks,), jnp.float32, least / len(shards), top_value / len(shards)))
        gain = gain * jnp.repeat(heights, dims[axis_at] // blocks).reshape([-1 if axis == axis_at else 1 for axis in range(len(dims))])
    return gain


def profile(amount, total, limit, lean):
    loads = [(1 << 20) // math.isqrt(grade ** lean) + 1 for grade in range(2, amount + 1)]
    spare, counts = total - limit - (amount - 1), [1] * (amount - 1)
    while spare > 0:
        candidates = [i for i in range(amount - 1) if counts[i] < limit]
        whole, budget = sum([loads[i] for i in candidates]), spare
        for i in candidates:
            more = min(limit - counts[i], max(1, budget * loads[i] // whole), spare)
            counts[i] = counts[i] + more
            spare = spare - more
    return np.array([limit] + counts)


def ragged_sizes(stream_key, amount, total, limit, skew):
    if amount == 2:
        one = jax.random.randint(stream_key, (), max(1, total - limit), min(limit, total - 1) + 1)
        return jnp.stack([one, total - one])
    tallies = jnp.asarray(profile(amount, total, limit, skew), jnp.int32)
    twos = (amount - 1) // 2
    donor, receiver = tallies[1:1 + 2 * twos:2], tallies[2:2 + 2 * twos:2]
    slack = jnp.minimum(donor - 1, limit - receiver)
    shifted = jax.random.randint(jax.random.fold_in(stream_key, 1), (twos,), 0, 1 << 20) % (slack + 1)
    tallies = tallies.at[1:1 + 2 * twos:2].set(donor - shifted).at[2:2 + 2 * twos:2].set(receiver + shifted)
    return tallies[jax.random.permutation(jax.random.fold_in(stream_key, 2), amount)]


def bell_draw(key, extent, scale, bound, pieces=(), held_as=jnp.bfloat16):
    drawn = jax.random.normal(key, extent, jnp.float32) * scale
    if len(pieces) > 0:
        drawn = level_of(key, extent, pieces, -0.22, 0.18) * drawn
    return jnp.clip(drawn, min=-bound, max=bound).astype(held_as)


def setup_inputs(seed: int = 0) -> dict:
    key_of = jax.random.split(jax.random.key(seed), 8)
    return {
        "events": bell_draw(key_of[0], (N_DP, SEQ, D), 1.0, 6.0, ((0, 8), (1, 32))),
        "lengths": jax.vmap(lambda own: ragged_sizes(own, USERS, NBLK, MAXB, 2))(jax.random.split(key_of[1], N_DP)).reshape((N_DP, USERS)).astype(jnp.int32),
        "block_slots": jax.vmap(lambda own: jax.random.permutation(own, NBLK))(jax.random.split(key_of[2], N_DP)).reshape((N_DP, NBLK)).astype(jnp.int32),
        "w_in": draw_w_in(jax.random.fold_in(key_of[7], 71), 0),
        "w_out": bell_draw(key_of[4], (D, D), D ** -0.5, 0.25),
        "w_pool": bell_draw(key_of[5], (D, 2 * D), D ** -0.5, 0.25, ((1, 8),)),
        "queries": bell_draw(key_of[6], (NQ, D), 1.0, 4.0),
    }


def layer_norm(values):
    centered_scores = values - lax.optimization_barrier(jnp.mean(values, axis=-1, keepdims=True))
    spread = lax.optimization_barrier(jnp.mean(centered_scores * centered_scores, axis=-1, keepdims=True))
    return centered_scores * lax.rsqrt(spread + 1e-05)

def rounded(values):
    return lax.optimization_barrier(values.astype(jnp.bfloat16)).astype(jnp.float32)

def one_group(events, lengths, block_slots, w_in, w_out, w_pool, queries):
    normed_in = layer_norm(events.astype(jnp.float32)).astype(jnp.bfloat16)
    proj = jax.nn.silu(jnp.dot(normed_in, w_in, preferred_element_type=jnp.float32))
    upper = proj[:, :D]
    values = rounded(proj[:, D:2 * D]).reshape(SEQ, H, HEAD_DIMENSION)
    query = rounded(proj[:, 2 * D:3 * D]).reshape(SEQ, H, HEAD_DIMENSION)
    keys = rounded(proj[:, 3 * D:]).reshape(SEQ, H, HEAD_DIMENSION)
    ends = jnp.cumsum(lengths).astype(jnp.int32) * BLOCK
    token_position = jnp.arange(SEQ, dtype=jnp.int32)
    owner = lax.optimization_barrier(jnp.sum((token_position[:, None] >= ends[None, :]).astype(jnp.int32), axis=1))
    span = MAXB * BLOCK

    def block_rows(index):
        first = (index * BLOCK).astype(jnp.int32)
        start = (jnp.maximum(index - MAXB + 1, 0) * BLOCK).astype(jnp.int32)
        qrows = lax.dynamic_slice_in_dim(query, first, BLOCK)
        krows = lax.dynamic_slice_in_dim(keys, start, span)
        vrows = lax.dynamic_slice_in_dim(values, start, span)
        qpos = lax.dynamic_slice_in_dim(token_position, first, BLOCK)
        kpos = lax.dynamic_slice_in_dim(token_position, start, span)
        quser = lax.dynamic_slice_in_dim(owner, first, BLOCK)
        kuser = lax.dynamic_slice_in_dim(owner, start, span)
        allowed = (kpos[None, :] <= qpos[:, None]) & (kuser[None, :] == quser[:, None])
        scores = jnp.einsum('qhd,khd->hqk', qrows, krows) / jnp.sqrt(jnp.float32(HEAD_DIMENSION))
        weight = rounded(jnp.where(allowed[None], jax.nn.silu(scores), 0.0))
        return jnp.einsum('hqk,khd->qhd', weight, vrows).reshape(BLOCK, D)
    attended = lax.map(block_rows, jnp.arange(NBLK, dtype=jnp.int32)).reshape(SEQ, D)
    mixed = (layer_norm(attended) * upper).astype(jnp.bfloat16)
    result = (events.astype(jnp.float32) + jnp.dot(mixed, w_out, preferred_element_type=jnp.float32)).astype(jnp.bfloat16)
    layer_out = result.reshape(NBLK, BLOCK, D)[block_slots].reshape(SEQ, D)
    pool_kv = jnp.dot(result, w_pool, preferred_element_type=jnp.float32)
    interest_key_rows = pool_kv[:, :D].reshape(SEQ, H, HEAD_DIMENSION)
    pool_values = pool_kv[:, D:].reshape(SEQ, H, HEAD_DIMENSION)
    requested_rows = queries.astype(jnp.float32).reshape(NQ, H, HEAD_DIMENSION)
    exponent_scores = jnp.exp(jnp.einsum('lzf,szf->lsz', interest_key_rows, requested_rows, precision=lax.Precision.HIGHEST) / jnp.sqrt(jnp.float32(HEAD_DIMENSION)))
    member = (owner[:, None] == jnp.arange(USERS, dtype=jnp.int32)[None, :]).astype(jnp.float32)
    totals = jnp.einsum('ru,rmh->umh', member, exponent_scores, precision=lax.Precision.HIGHEST)
    weighted = jnp.einsum('ru,rmh,rhd->umhd', member, exponent_scores, pool_values, precision=lax.Precision.HIGHEST)
    interests = (weighted / totals[..., None]).reshape(USERS, NQ, D)
    return (layer_out, interests)

def reference(events, lengths, block_slots, w_in, w_out, w_pool, queries):
    outputs = []
    pooled = []
    for group in range(N_DP):
        layer_out, interests = one_group(events[group], lengths[group], block_slots[group], w_in, w_out, w_pool, queries)
        outputs.append(layer_out)
        pooled.append(interests)
    return (jnp.stack(outputs), jnp.stack(pooled))
```

```python
import functools

import jax
import jax.numpy as jnp
from jax import lax
from jax.experimental import pallas as pl
from jax.experimental.pallas import tpu as pltpu
from jax.sharding import PartitionSpec as P

D = 512
H = 4
HD = 128
NQ = 8
BLOCK = 256
USERS = 4
NX = 4
NZ = 8
NC = NX * NZ
SHIFT = 8
PIECE = BLOCK // NC
WIDE = D + HD
F32 = jnp.float32
BF16 = jnp.bfloat16
HALF_SCALE = 0.5 / (HD**0.5)


def normed(values):
    centered = values - jnp.mean(values, axis=-1, keepdims=True)
    spread = jnp.mean(centered * centered, axis=-1, keepdims=True)
    return centered * lax.rsqrt(spread + 1e-05)


def silu_of_twice(half):
    return half + half * jnp.tanh(half)


def project(rows, weight):
    return silu_of_twice(0.5 * jnp.dot(rows, weight, preferred_element_type=F32))


def place_in_user(lengths_ref, block):
    end = lengths_ref[0, 0]
    user = jnp.int32(0)
    start = jnp.int32(0)
    for other in range(USERS - 1):
        past = block >= end
        user = jnp.where(past, other + 1, user)
        start = jnp.where(past, end, start)
        end = end + lengths_ref[0, other + 1]
    return user, block - start


def offsets(x):
    out = []
    for row, turn in WINDOW:
        column = lax.rem(x + turn, NX)
        if row == 2:
            out.append(jnp.where(column <= x, x - column, 16 - (column - x)))
        else:
            out.append(8 - 4 * row - (column - x))
    return out


WINDOW = [(row, turn) for row in (2, 0, 1, -1) for turn in (0, 3, 1, 2)]


def layer_kernel(*refs):
    lengths_ref = refs[0]
    blocks = refs[1:17]
    (w_ref, out_w_ref, pool_ref, ask_ref, send_ref, held, acc, q_ref, u_ref, sems) = refs[17:]
    place = lax.axis_index("ctx")
    x = lax.rem(place, NX)
    block = lax.rem(place + SHIFT, NC)
    _, before = place_in_user(lengths_ref, block)
    steps_back = offsets(x)
    copies = []
    for ref, back in zip(blocks, steps_back):
        wanted = back <= before
        copy = pltpu.make_async_copy(ref, held.at[back], sems.at[back])
        copies.append(copy)

        @pl.when(wanted)
        def _(copy=copy):
            copy.start()

    def wait(back):
        pltpu.make_async_copy(blocks[0], held.at[back], sems.at[back]).wait()

    def keys_values(back):
        rows = normed(held[back].astype(F32)).astype(BF16)
        values = [project(rows, w_ref[i]).astype(BF16) for i in (2, 3)]
        keys = [project(rows, w_ref[i]).astype(BF16) for i in (6, 7)]
        return rows, keys, values

    def head(pair, h):
        return pair[h // 2][:, (h % 2) * HD : (h % 2 + 1) * HD]

    def attend(query, keys, values, h, mask=None):
        scores = lax.dot_general(
            query, head(keys, h), (((1,), (1,)), ((), ())), preferred_element_type=F32
        )
        weight = silu_of_twice(scores * HALF_SCALE)
        if mask is not None:
            weight = jnp.where(mask, weight, 0.0)
        return jnp.dot(weight.astype(BF16), head(values, h), preferred_element_type=F32)

    wait(0)
    rows, keys, values = keys_values(0)
    queries = [project(rows, w_ref[i]).astype(BF16) for i in (4, 5)]
    for half in range(2):
        q_ref[:, half * 256 : (half + 1) * 256] = queries[half]
        u_ref[:, half * 256 : (half + 1) * 256] = project(rows, w_ref[half])
    mask = lax.broadcasted_iota(jnp.int32, (BLOCK, BLOCK), 1) <= lax.broadcasted_iota(
        jnp.int32, (BLOCK, BLOCK), 0
    )
    for h in range(H):
        acc[:, h * HD : (h + 1) * HD] = attend(head(queries, h), keys, values, h, mask)

    def one_block(back, carry):
        wait(back)
        _, keys, values = keys_values(back)
        for h in range(H):
            acc[:, h * HD : (h + 1) * HD] += attend(
                q_ref[:, h * HD : (h + 1) * HD], keys, values, h
            )
        return carry

    lax.fori_loop(1, before + 1, one_block, 0)

    mixed = (normed(acc[...]) * u_ref[...]).astype(BF16)
    result = held[0].astype(F32) + jnp.dot(mixed, out_w_ref[...], preferred_element_type=F32)
    result = result.astype(BF16)
    wide = result.astype(F32)
    for i in range(NC):
        send_ref[i, :, :D] = wide[i * PIECE : (i + 1) * PIECE].astype(BF16)
    row = lax.broadcasted_iota(jnp.int32, (8, HD), 0)
    for h in range(H):
        key = jnp.dot(result, pool_ref[h], preferred_element_type=F32)
        value = jnp.dot(result, pool_ref[H + h], preferred_element_type=F32)
        ask = ask_ref[:, h * HD : (h + 1) * HD].astype(F32)
        scores = lax.dot_general(
            ask,
            key,
            (((1,), (1,)), ((), ())),
            precision=lax.Precision.HIGHEST,
            preferred_element_type=F32,
        )
        expo = jnp.exp(scores / (HD**0.5))
        total = jnp.sum(expo, axis=1, keepdims=True)
        weighted = jnp.dot(
            expo, value, precision=lax.Precision.HIGHEST, preferred_element_type=F32
        )
        total = jnp.broadcast_to(total, (NQ, HD))
        weighted_top = weighted.astype(BF16).astype(F32)
        total_top = total.astype(BF16).astype(F32)
        for m in range(NQ):
            tile = jnp.where(row == 0, weighted_top[m : m + 1], 0.0)
            tile = jnp.where(row == 1, (weighted - weighted_top)[m : m + 1], tile)
            tile = jnp.where(row == 2, total_top[m : m + 1], tile)
            tile = jnp.where(row == 3, (total - total_top)[m : m + 1], tile)
            send_ref[m * H + h, :, D:] = tile.astype(BF16)


def turn_kernel(lengths_ref, slots_ref, got_ref, send_ref, sums):
    sums[...] = jnp.zeros_like(sums)
    for j in range(NC):
        user, _ = place_in_user(lengths_ref, jnp.int32((j + SHIFT) % NC))
        sums[user] += got_ref[j, :, D:].astype(F32)
    row = lax.broadcasted_iota(jnp.int32, (8, HD), 0)
    tile = jnp.zeros((8, HD), F32)
    for user in range(USERS):
        part = sums[user]
        mean = (part[0:1] + part[1:2]) / (part[2:3] + part[3:4])
        top = mean.astype(BF16).astype(F32)
        tile = jnp.where(row == user, top, tile)
        tile = jnp.where(row == user + USERS, mean - top, tile)
    tile = tile.astype(BF16)
    for s in range(NC):
        source = lax.rem(slots_ref[0, s] + (NC - SHIFT), NC)
        send_ref[s, :, :D] = got_ref[source, :, :D]
        send_ref[s, :, D:] = tile


def last_kernel(got_ref, out_ref, interests_ref):
    for i in range(0, NC, 2):
        pair = jnp.concatenate(
            [got_ref[i, :, :D].astype(F32), got_ref[i + 1, :, :D].astype(F32)], axis=0
        )
        out_ref[0, i * PIECE : (i + 2) * PIECE, :] = pair.astype(BF16)
    for m in range(NQ):
        for h in range(H):
            tile = got_ref[m * H + h, :, D:].astype(F32)
            mean = tile[:USERS] + tile[USERS:]
            for user in range(USERS):
                interests_ref[0, user, m : m + 1, h * HD : (h + 1) * HD] = mean[user : user + 1]


def move(values, dz, dx):
    pairs = []
    for z in range(NZ):
        for x in range(NX):
            pairs.append((z * NX + x, ((z + dz) % NZ) * NX + (x + dx) % NX))
    return lax.ppermute(values, "ctx", pairs)


def shards(events, lengths, block_slots, w_in, w_out, w_pool, queries):
    own = events[0]
    full_in = lax.all_gather(w_in, "dp", axis=0)
    full_pool = lax.all_gather(w_pool, "dp", axis=0)
    up = move(own, -1, 0)
    down = move(own, 1, 0)
    row = {0: own, 3: move(own, 0, 1), 1: move(own, 0, -1), 2: move(own, 0, 2)}
    up2 = move(up, -1, 0)
    down2 = move(down, 1, 0)
    x = lax.rem(lax.axis_index("ctx"), NX)
    far = {0: up2}
    for turn in (3, 1, 2):
        target = lax.rem(x + NX - turn, NX)
        far[turn] = move(jnp.where(x <= target, up2, down2), 0, -turn)
    window = {}
    for turn in range(NX):
        window[2, turn] = far[turn]
        window[0, turn] = row[turn]
        window[1, turn] = up if turn == 0 else move(row[turn], -1, 0)
        window[-1, turn] = down if turn == 0 else move(row[turn], 1, 0)
    smem = pl.BlockSpec(memory_space=pltpu.SMEM)
    vmem = pl.BlockSpec(memory_space=pltpu.VMEM)
    params = pltpu.CompilerParams(vmem_limit_bytes=40 * 1024 * 1024)
    send = pl.pallas_call(
        layer_kernel,
        out_shape=jax.ShapeDtypeStruct((NC, PIECE, WIDE), BF16),
        in_specs=[smem] + [pl.BlockSpec(memory_space=pl.ANY)] * 16 + [vmem] * 4,
        out_specs=vmem,
        scratch_shapes=[
            pltpu.VMEM((16, BLOCK, D), BF16),
            pltpu.VMEM((BLOCK, D), F32),
            pltpu.VMEM((BLOCK, D), BF16),
            pltpu.VMEM((BLOCK, D), F32),
            pltpu.SemaphoreType.DMA((16,)),
        ],
        compiler_params=params,
        name="layer",
    )(lengths, *[window[key] for key in WINDOW], full_in, w_out, full_pool, queries)
    got = lax.all_to_all(send, "ctx", 0, 0, tiled=True)
    send = pl.pallas_call(
        turn_kernel,
        out_shape=jax.ShapeDtypeStruct((NC, PIECE, WIDE), BF16),
        in_specs=[smem, smem, vmem],
        out_specs=vmem,
        scratch_shapes=[pltpu.VMEM((USERS, 8, HD), F32)],
        compiler_params=params,
        name="turn",
    )(lengths, block_slots, got)
    got = lax.all_to_all(send, "ctx", 0, 0, tiled=True)
    return pl.pallas_call(
        last_kernel,
        out_shape=(
            jax.ShapeDtypeStruct((1, BLOCK, D), BF16),
            jax.ShapeDtypeStruct((1, USERS, NQ, D), F32),
        ),
        in_specs=[vmem],
        out_specs=(vmem, vmem),
        compiler_params=params,
        name="last",
    )(got)


def solution(mesh):
    in_specs = (
        P("dp", "ctx", None),
        P("dp", None),
        P("dp", None),
        P(None, "dp"),
        P(),
        P(None, "dp"),
        P(),
    )
    out_specs = (P("dp", "ctx", None), P("dp", None, None, None))
    return jax.shard_map(shards, mesh=mesh, in_specs=in_specs, out_specs=out_specs, check_vma=False)
```

```python
import functools

import jax
import jax.numpy as jnp
from jax import lax
from jax.experimental import pallas as pl
from jax.experimental.pallas import tpu as pltpu
from jax.sharding import PartitionSpec as P

D = 512
H = 4
HD = 128
NQ = 8
BLOCK = 256
USERS = 4
NX = 4
NZ = 8
NC = NX * NZ
SHIFT = 8
AHEAD = SHIFT // NX
ROWS = 5
COLS = 256
POOL = 128
PIECE = BLOCK // NC
WIDE = D + HD
F32 = jnp.float32
BF16 = jnp.bfloat16
HALF_SCALE = 0.5 / (HD**0.5)


def normed(values):
    centered = values - jnp.mean(values, axis=-1, keepdims=True)
    spread = jnp.mean(centered * centered, axis=-1, keepdims=True)
    return centered * lax.rsqrt(spread + 1e-05)


def silu_of_twice(half):
    return half + half * jnp.tanh(half)


def project(rows, weight):
    return silu_of_twice(0.5 * jnp.dot(rows, weight, preferred_element_type=F32))


def place_in_user(lengths_ref, block):
    end = lengths_ref[0, 0]
    user = jnp.int32(0)
    start = jnp.int32(0)
    for other in range(USERS - 1):
        past = block >= end
        user = jnp.where(past, other + 1, user)
        start = jnp.where(past, end, start)
        end = end + lengths_ref[0, other + 1]
    return user, block - start


def my_place():
    place = lax.axis_index("ctx")
    lane = lax.axis_index("dp")
    return lax.div(place, NX), lax.rem(place, NX), lax.div(lane, 2), lax.rem(lane, 2)


def head(h):
    return slice(h * HD, (h + 1) * HD)


def prepare_kernel(*refs):
    shards_in, blocks = refs[:8], refs[8:13]
    w_ref, keys_ref, values_ref, sems = refs[13:]
    _, _, y, core = my_place()
    side = 1 - 2 * core
    copies = []
    for i, ref in enumerate(shards_in):
        there = core if i < 4 else 1 - core
        step = (0, -1, 1, 2)[i % 4]
        turn = side if i < 4 else -side
        slot = 2 * lax.rem(y + 4 + step * turn, 4) + there
        copy = pltpu.make_async_copy(ref, w_ref.at[slot], sems.at[i])
        copy.start()
        copies.append(copy)
    for copy in copies:
        copy.wait()
    for j, block in enumerate(blocks):
        rows = normed(block[...].astype(F32)).astype(BF16)
        for half in range(2):
            part = slice(half * COLS, (half + 1) * COLS)
            values_ref[j, :, part] = project(rows, w_ref[2 + half, :, :COLS]).astype(BF16)
            keys_ref[j, :, part] = project(rows, w_ref[6 + half, :, :COLS]).astype(BF16)


def attend_kernel(source, *refs):
    own = source == "own"
    lengths_ref, events_ref, w_ref, keys_ref, values_ref, out_ref = refs[:6]
    if own:
        u_ref, acc = refs[6:]
    else:
        (acc,) = refs[6:]
    z, x, _, core = my_place()
    turn = {"own": 0, "first": 3 - 2 * core, "second": 1 + 2 * core, "third": 2}[source]
    column = lax.rem(x + turn, NX)
    block = NX * lax.rem(z + AHEAD, NZ) + column
    _, before = place_in_user(lengths_ref, block)
    skip = jnp.where(column >= x, 0, 1)
    nearest = column - x + NX * skip
    count = jnp.where(before >= nearest, lax.div(before - nearest, NX) + 1, 0)

    rows = normed(events_ref[...].astype(F32)).astype(BF16)
    queries = [project(rows, w_ref[4 + half, :, :COLS]).astype(BF16) for half in range(2)]
    if own:
        for half in range(2):
            u_ref[:, half * COLS : (half + 1) * COLS] = project(rows, w_ref[half, :, :COLS])

    def one_head(j, h, masked):
        query = queries[h // 2][:, head(h % 2)]
        scores = lax.dot_general(
            query, keys_ref[j, :, head(h)], (((1,), (1,)), ((), ())), preferred_element_type=F32
        )
        weight = silu_of_twice(scores * HALF_SCALE)
        if masked:
            later = lax.broadcasted_iota(jnp.int32, (BLOCK, BLOCK), 1)
            weight = jnp.where(later <= lax.broadcasted_iota(jnp.int32, (BLOCK, BLOCK), 0), weight, 0.0)
        return jnp.dot(weight.astype(BF16), values_ref[j, :, head(h)], preferred_element_type=F32)

    @pl.when(count == 4)
    def _():
        for h in range(H):
            total = one_head(skip, h, own)
            for j in range(1, 4):
                total = total + one_head(skip + j, h, False)
            acc[:, head(h)] = total

    @pl.when(count < 4)
    def _():
        for h in range(H):
            if own:
                acc[:, head(h)] = one_head(0, h, True)
            else:
                acc[:, head(h)] = jnp.zeros((BLOCK, HD), F32)

        def step(j, carry):
            for h in range(H):
                acc[:, head(h)] += one_head(skip + j, h, False)
            return carry

        lax.fori_loop(1 if own else 0, count, step, 0)

    out_ref[...] = acc[...].astype(out_ref.dtype)


def finish_kernel(*refs):
    events_ref, u_ref = refs[:2]
    parts = refs[2:6]
    out_w_ref, w_ref, ask_ref, send_ref = refs[6:]
    attended = parts[0][...]
    for part in parts[1:]:
        attended = attended + part[...].astype(F32)
    mixed = (normed(attended) * u_ref[...]).astype(BF16)
    result = events_ref[...].astype(F32) + jnp.dot(
        mixed, out_w_ref[...], preferred_element_type=F32
    )
    result = result.astype(BF16)
    wide = result.astype(F32)
    for i in range(NC):
        send_ref[i, :, :D] = wide[i * PIECE : (i + 1) * PIECE].astype(BF16)
    row = lax.broadcasted_iota(jnp.int32, (8, HD), 0)
    for h in range(H):
        key = jnp.dot(result, w_ref[h, :, COLS:], preferred_element_type=F32)
        value = jnp.dot(result, w_ref[H + h, :, COLS:], preferred_element_type=F32)
        ask = ask_ref[:, head(h)].astype(F32)
        scores = lax.dot_general(
            ask,
            key,
            (((1,), (1,)), ((), ())),
            precision=lax.Precision.HIGHEST,
            preferred_element_type=F32,
        )
        expo = jnp.exp(scores / (HD**0.5))
        total = jnp.sum(expo, axis=1, keepdims=True)
        weighted = jnp.dot(
            expo, value, precision=lax.Precision.HIGHEST, preferred_element_type=F32
        )
        total = jnp.broadcast_to(total, (NQ, HD))
        weighted_top = weighted.astype(BF16).astype(F32)
        total_top = total.astype(BF16).astype(F32)
        for m in range(NQ):
            tile = jnp.where(row == 0, weighted_top[m : m + 1], 0.0)
            tile = jnp.where(row == 1, (weighted - weighted_top)[m : m + 1], tile)
            tile = jnp.where(row == 2, total_top[m : m + 1], tile)
            tile = jnp.where(row == 3, (total - total_top)[m : m + 1], tile)
            send_ref[m * H + h, :, D:] = tile.astype(BF16)


def turn_kernel(lengths_ref, slots_ref, got_ref, send_ref, sums):
    sums[...] = jnp.zeros_like(sums)
    for j in range(NC):
        user, _ = place_in_user(lengths_ref, jnp.int32((j + SHIFT) % NC))
        sums[user] += got_ref[j, :, D:].astype(F32)
    row = lax.broadcasted_iota(jnp.int32, (8, HD), 0)
    tile = jnp.zeros((8, HD), F32)
    for user in range(USERS):
        part = sums[user]
        mean = (part[0:1] + part[1:2]) / (part[2:3] + part[3:4])
        top = mean.astype(BF16).astype(F32)
        tile = jnp.where(row == user, top, tile)
        tile = jnp.where(row == user + USERS, mean - top, tile)
    tile = tile.astype(BF16)
    for s in range(NC):
        source = lax.rem(slots_ref[0, s] + (NC - SHIFT), NC)
        send_ref[s, :, :D] = got_ref[source, :, :D]
        send_ref[s, :, D:] = tile


def last_kernel(got_ref, out_ref, interests_ref):
    for i in range(0, NC, 2):
        pair = jnp.concatenate(
            [got_ref[i, :, :D].astype(F32), got_ref[i + 1, :, :D].astype(F32)], axis=0
        )
        out_ref[0, i * PIECE : (i + 2) * PIECE, :] = pair.astype(BF16)
    for m in range(NQ):
        for h in range(H):
            tile = got_ref[m * H + h, :, D:].astype(F32)
            mean = tile[:USERS] + tile[USERS:]
            for user in range(USERS):
                interests_ref[0, user, m : m + 1, h * HD : (h + 1) * HD] = mean[user : user + 1]


def move_ctx(values, dz, dx):
    pairs = []
    for z in range(NZ):
        for x in range(NX):
            pairs.append((z * NX + x, ((z + dz) % NZ) * NX + (x + dx) % NX))
    return lax.ppermute(values, "ctx", pairs)


def move_x(values, dx):
    pairs = []
    for lane in range(8):
        for z in range(NZ):
            for x in range(NX):
                there = (x + (dx if lane % 2 == 0 else -dx)) % NX
                pairs.append((lane * NC + z * NX + x, lane * NC + z * NX + there))
    return lax.ppermute(values, ("dp", "ctx"), pairs)


def move_y(values, dy):
    pairs = []
    for y in range(4):
        for core in range(2):
            there = (y + (dy if core == 0 else -dy)) % 4
            pairs.append((2 * y + core, 2 * there + core))
    return lax.ppermute(values, "dp", pairs)


def swap_cores(values):
    return lax.ppermute(values, "dp", [(lane, lane ^ 1) for lane in range(8)])


def shards(events, lengths, block_slots, w_in, w_out, w_pool, queries):
    own = events[0]
    weights = jnp.concatenate([w_in, w_pool], axis=1)
    up = move_ctx(own, -1, 0)
    down = move_ctx(own, 1, 0)
    weights_a = move_y(weights, 1)
    weights_b = move_y(weights, -1)
    up2 = move_ctx(up, -1, 0)
    down2 = move_ctx(down, 1, 0)
    weights_c = move_y(weights_a, 1)
    mine = [weights, weights_a, weights_b, weights_c]
    pieces = mine + [swap_cores(one) for one in mine]
    first = move_x(up2, 1)
    second = move_x(up2, -1)
    third = move_x(first, 1)
    smem = pl.BlockSpec(memory_space=pltpu.SMEM)
    vmem = pl.BlockSpec(memory_space=pltpu.VMEM)
    params = pltpu.CompilerParams(vmem_limit_bytes=16 * 1024 * 1024)
    shape = jax.ShapeDtypeStruct
    w_all, keys, values = pl.pallas_call(
        prepare_kernel,
        out_shape=(
            shape((8, D, COLS + POOL), BF16),
            shape((ROWS, BLOCK, D), BF16),
            shape((ROWS, BLOCK, D), BF16),
        ),
        in_specs=[pl.BlockSpec(memory_space=pl.ANY)] * 8 + [vmem] * ROWS,
        out_specs=(vmem, vmem, vmem),
        scratch_shapes=[pltpu.SemaphoreType.DMA((8,))],
        compiler_params=params,
        name="prepare",
    )(*pieces, up2, up, own, down, down2)

    def attend(source, block):
        out = shape((BLOCK, D), F32 if source == "own" else BF16)
        return pl.pallas_call(
            functools.partial(attend_kernel, source),
            out_shape=(out, shape((BLOCK, D), F32)) if source == "own" else out,
            in_specs=[smem] + [vmem] * 4,
            out_specs=(vmem, vmem) if source == "own" else vmem,
            scratch_shapes=[pltpu.VMEM((BLOCK, D), F32)],
            compiler_params=params,
            name="attend_" + source,
        )(lengths, block, w_all, keys, values)

    first = move_x(attend("first", first), -1)
    second = move_x(attend("second", second), 1)
    third = move_ctx(attend("third", third), 0, 2)
    attended, u = attend("own", up2)
    send = pl.pallas_call(
        finish_kernel,
        out_shape=shape((NC, PIECE, WIDE), BF16),
        in_specs=[vmem] * 9,
        out_specs=vmem,
        compiler_params=params,
        name="finish",
    )(up2, u, attended, first, second, third, w_out, w_all, queries)
    got = lax.all_to_all(send, "ctx", 0, 0, tiled=True)
    send = pl.pallas_call(
        turn_kernel,
        out_shape=shape((NC, PIECE, WIDE), BF16),
        in_specs=[smem, smem, vmem],
        out_specs=vmem,
        scratch_shapes=[pltpu.VMEM((USERS, 8, HD), F32)],
        compiler_params=params,
        name="turn",
    )(lengths, block_slots, got)
    got = lax.all_to_all(send, "ctx", 0, 0, tiled=True)
    return pl.pallas_call(
        last_kernel,
        out_shape=(shape((1, BLOCK, D), BF16), shape((1, USERS, NQ, D), F32)),
        in_specs=[vmem],
        out_specs=(vmem, vmem),
        compiler_params=params,
        name="last",
    )(got)


def solution(mesh):
    in_specs = (
        P("dp", "ctx", None),
        P("dp", None),
        P("dp", None),
        P(None, "dp"),
        P(),
        P(None, "dp"),
        P(),
    )
    out_specs = (P("dp", "ctx", None), P("dp", None, None, None))
    return jax.shard_map(shards, mesh=mesh, in_specs=in_specs, out_specs=out_specs, check_vma=False)
```

```python
import functools

import jax
import jax.numpy as jnp
from jax import lax
from jax.experimental import pallas as pl
from jax.experimental.pallas import tpu as pltpu
from jax.sharding import PartitionSpec as P

D = 512
H = 4
HD = 128
NQ = 8
BLOCK = 256
USERS = 4
NX = 4
NZ = 8
NC = NX * NZ
AHEAD = 2
SHIFT = AHEAD * NX
ROWS = 5
COLS = 256
POOL = 128
PIECE = BLOCK // NC
WIDE = D + HD
F32 = jnp.float32
BF16 = jnp.bfloat16
HALF_SCALE = 0.5 / (HD**0.5)


def normed(values):
    centered = values - jnp.mean(values, axis=-1, keepdims=True)
    spread = jnp.mean(centered * centered, axis=-1, keepdims=True)
    return centered * lax.rsqrt(spread + 1e-05)


def silu_of_twice(half):
    return half + half * jnp.tanh(half)


def project(rows, weight):
    return silu_of_twice(0.5 * jnp.dot(rows, weight, preferred_element_type=F32))


def place_in_user(lengths_ref, block):
    end = lengths_ref[0, 0]
    user = jnp.int32(0)
    start = jnp.int32(0)
    for other in range(USERS - 1):
        past = block >= end
        user = jnp.where(past, other + 1, user)
        start = jnp.where(past, end, start)
        end = end + lengths_ref[0, other + 1]
    return user, block - start


def my_place():
    place = lax.axis_index("ctx")
    lane = lax.axis_index("dp")
    return lax.div(place, NX), lax.rem(place, NX), lax.div(lane, 2), lax.rem(lane, 2)


def head(h):
    return slice(h * HD, (h + 1) * HD)


def keys_values(events, w_ref, keys_ref, values_ref, j):
    rows = normed(events.astype(F32)).astype(BF16)
    for half in range(2):
        part = slice(half * COLS, (half + 1) * COLS)
        values_ref[j, :, part] = project(rows, w_ref[2 + half, :, :COLS]).astype(BF16)
        keys_ref[j, :, part] = project(rows, w_ref[6 + half, :, :COLS]).astype(BF16)
    return rows


def prepare_kernel(*refs):
    shards_in, blocks = refs[:8], refs[8:13]
    w_ref, keys_ref, values_ref, q_ref, u_ref, sems = refs[-6:]
    _, _, y, core = my_place()
    side = 1 - 2 * core
    copies = []
    for i, ref in enumerate(shards_in):
        there = core if i < 4 else 1 - core
        step = (0, -1, 1, 2)[i % 4]
        turn = side if i < 4 else -side
        slot = 2 * lax.rem(y + 4 + step * turn, 4) + there
        copy = pltpu.make_async_copy(ref, w_ref.at[slot], sems.at[i])
        copy.start()
        copies.append(copy)
    for copy in copies:
        copy.wait()
    for j, block in enumerate(blocks):
        rows = keys_values(block[...], w_ref, keys_ref, values_ref, j)
        if j == 0:
            for half in range(2):
                part = slice(half * COLS, (half + 1) * COLS)
                q_ref[:, part] = project(rows, w_ref[4 + half, :, :COLS]).astype(BF16)
                u_ref[:, part] = project(rows, w_ref[half, :, :COLS])


def attend_kernel(source, *refs):
    own = source == "own"
    lengths_ref, events_ref, w_ref, keys_ref, values_ref = refs[:5]
    out_ref, acc = refs[-2:]
    if own:
        ask_ref, ask_out_ref = refs[5:7]
        for h in range(H):
            ask = lax.dot_general(
                ask_ref[:, head(h)],
                w_ref[h, :, COLS:],
                (((1,), (1,)), ((), ())),
                preferred_element_type=F32,
            )
            top = ask.astype(BF16).astype(F32)
            ask_out_ref[h * NQ : (h + 1) * NQ, :] = top
            ask_out_ref[(H + h) * NQ : (H + h + 1) * NQ, :] = ask - top
    z, x, _, core = my_place()
    turn = {"own": 0, "first": 3 - 2 * core, "second": 1 + 2 * core, "third": 2}[source]
    column = lax.rem(x + turn, NX)
    block = NX * lax.rem(z + AHEAD, NZ) + column
    _, before = place_in_user(lengths_ref, block)
    skip = jnp.where(column >= x, 0, 1)
    nearest = column - x + NX * skip
    count = jnp.where(before >= nearest, lax.div(before - nearest, NX) + 1, 0)

    if own:
        queries = [events_ref[:, half * COLS : (half + 1) * COLS] for half in range(2)]
    else:
        rows = normed(events_ref[...].astype(F32)).astype(BF16)
        queries = [project(rows, w_ref[4 + half, :, :COLS]).astype(BF16) for half in range(2)]

    def one_head(j, h, masked):
        query = queries[h // 2][:, head(h % 2)]
        scores = lax.dot_general(
            query, keys_ref[j, :, head(h)], (((1,), (1,)), ((), ())), preferred_element_type=F32
        )
        weight = silu_of_twice(scores * HALF_SCALE)
        if masked:
            later = lax.broadcasted_iota(jnp.int32, (BLOCK, BLOCK), 1)
            weight = jnp.where(later <= lax.broadcasted_iota(jnp.int32, (BLOCK, BLOCK), 0), weight, 0.0)
        return jnp.dot(weight.astype(BF16), values_ref[j, :, head(h)], preferred_element_type=F32)

    @pl.when(count == 4)
    def _():
        for h in range(H):
            total = one_head(skip, h, own)
            for j in range(1, 4):
                total = total + one_head(skip + j, h, False)
            acc[:, head(h)] = total

    @pl.when(count < 4)
    def _():
        for h in range(H):
            if own:
                acc[:, head(h)] = one_head(0, h, True)
            else:
                acc[:, head(h)] = jnp.zeros((BLOCK, HD), F32)

        def step(j, carry):
            for h in range(H):
                acc[:, head(h)] += one_head(skip + j, h, False)
            return carry

        lax.fori_loop(1 if own else 0, count, step, 0)

    out_ref[...] = acc[...].astype(out_ref.dtype)


def finish_kernel(*refs):
    events_ref, u_ref = refs[:2]
    parts = refs[2:6]
    out_w_ref, w_ref, ask_ref, send_ref = refs[6:]
    attended = parts[0][...]
    for part in parts[1:]:
        attended = attended + part[...].astype(F32)
    mixed = (normed(attended) * u_ref[...]).astype(BF16)
    result = events_ref[...].astype(F32) + jnp.dot(
        mixed, out_w_ref[...], preferred_element_type=F32
    )
    result = result.astype(BF16)
    wide = result.astype(F32)
    for i in range(NC):
        send_ref[i, :, :D] = wide[i * PIECE : (i + 1) * PIECE].astype(BF16)
    scores = lax.dot_general(
        ask_ref[...].astype(BF16), result, (((1,), (1,)), ((), ())), preferred_element_type=F32
    )
    expo = jnp.exp((scores[: H * NQ] + scores[H * NQ :]) / (HD**0.5))
    top = expo.astype(BF16)
    both = jnp.concatenate([top, (expo - top.astype(F32)).astype(BF16)], axis=0)
    totals = jnp.broadcast_to(jnp.sum(expo, axis=1, keepdims=True), (H * NQ, HD))
    row = lax.broadcasted_iota(jnp.int32, (8, HD), 0)
    for h in range(H):
        value = jnp.dot(result, w_ref[H + h, :, COLS:], preferred_element_type=F32)
        value_top = value.astype(BF16)
        value_low = (value - value_top.astype(F32)).astype(BF16)
        mine = jnp.concatenate(
            [both[h * NQ : (h + 1) * NQ], both[(H + h) * NQ : (H + h + 1) * NQ]], axis=0
        )
        weighted = jnp.dot(mine, value_top, preferred_element_type=F32)
        weighted = weighted + jnp.dot(mine, value_low, preferred_element_type=F32)
        weighted = weighted[:NQ] + weighted[NQ:]
        total = totals[h * NQ : (h + 1) * NQ]
        weighted_top = weighted.astype(BF16).astype(F32)
        total_top = total.astype(BF16).astype(F32)
        for m in range(NQ):
            tile = jnp.where(row == 0, weighted_top[m : m + 1], 0.0)
            tile = jnp.where(row == 1, (weighted - weighted_top)[m : m + 1], tile)
            tile = jnp.where(row == 2, total_top[m : m + 1], tile)
            tile = jnp.where(row == 3, (total - total_top)[m : m + 1], tile)
            send_ref[m * H + h, :, D:] = tile.astype(BF16)


def turn_kernel(lengths_ref, slots_ref, got_ref, send_ref, sums):
    sums[...] = jnp.zeros_like(sums)
    for j in range(NC):
        user, _ = place_in_user(lengths_ref, jnp.int32((j + SHIFT) % NC))
        sums[user] += got_ref[j, :, D:].astype(F32)
    row = lax.broadcasted_iota(jnp.int32, (8, HD), 0)
    tile = jnp.zeros((8, HD), F32)
    for user in range(USERS):
        part = sums[user]
        mean = (part[0:1] + part[1:2]) / (part[2:3] + part[3:4])
        top = mean.astype(BF16).astype(F32)
        tile = jnp.where(row == user, top, tile)
        tile = jnp.where(row == user + USERS, mean - top, tile)
    tile = tile.astype(BF16)
    for s in range(NC):
        source = lax.rem(slots_ref[0, s] + (NC - SHIFT), NC)
        send_ref[s, :, :D] = got_ref[source, :, :D]
        send_ref[s, :, D:] = tile


def last_kernel(got_ref, out_ref, interests_ref):
    for i in range(0, NC, 2):
        pair = jnp.concatenate(
            [got_ref[i, :, :D].astype(F32), got_ref[i + 1, :, :D].astype(F32)], axis=0
        )
        out_ref[0, i * PIECE : (i + 2) * PIECE, :] = pair.astype(BF16)
    for m in range(NQ):
        for h in range(H):
            tile = got_ref[m * H + h, :, D:].astype(F32)
            mean = tile[:USERS] + tile[USERS:]
            for user in range(USERS):
                interests_ref[0, user, m : m + 1, h * HD : (h + 1) * HD] = mean[user : user + 1]


def move_ctx(values, dz, dx):
    pairs = []
    for z in range(NZ):
        for x in range(NX):
            pairs.append((z * NX + x, ((z + dz) % NZ) * NX + (x + dx) % NX))
    return lax.ppermute(values, "ctx", pairs)


def move_x(values, dx):
    pairs = []
    for lane in range(8):
        for z in range(NZ):
            for x in range(NX):
                there = (x + (dx if lane % 2 == 0 else -dx)) % NX
                pairs.append((lane * NC + z * NX + x, lane * NC + z * NX + there))
    return lax.ppermute(values, ("dp", "ctx"), pairs)


def move_y(values, dy):
    pairs = []
    for y in range(4):
        for core in range(2):
            there = (y + (dy if core == 0 else -dy)) % 4
            pairs.append((2 * y + core, 2 * there + core))
    return lax.ppermute(values, "dp", pairs)


def swap_cores(values):
    return lax.ppermute(values, "dp", [(lane, lane ^ 1) for lane in range(8)])


def shards(events, lengths, block_slots, w_in, w_out, w_pool, queries):
    own = events[0]
    smem = pl.BlockSpec(memory_space=pltpu.SMEM)
    vmem = pl.BlockSpec(memory_space=pltpu.VMEM)
    free = pl.BlockSpec(memory_space=pl.ANY)
    params = pltpu.CompilerParams(vmem_limit_bytes=16 * 1024 * 1024)
    shape = jax.ShapeDtypeStruct
    some = lengths[0, 0] > 0
    up = move_ctx(own, -1, 0)
    down = move_ctx(own, 1, 0)
    up2 = move_ctx(jnp.where(some, up, down), -1, 0)
    down2 = move_ctx(down, 1, 0)
    asked = up2
    weights = jnp.concatenate([w_in, w_pool], axis=1)
    weights_a = move_y(weights, 1)
    weights_b = move_y(weights, -1)
    first = move_x(asked, 1)
    second = move_x(asked, -1)
    third = move_ctx(asked, 0, 2)
    weights_c = move_y(weights_a, 1)
    mine = [weights, weights_a, weights_b, weights_c]
    pieces = mine + [swap_cores(one) for one in mine]
    w_all, keys, values, q, u = pl.pallas_call(
        prepare_kernel,
        out_shape=(
            shape((8, D, COLS + POOL), BF16),
            shape((ROWS, BLOCK, D), BF16),
            shape((ROWS, BLOCK, D), BF16),
            shape((BLOCK, D), BF16),
            shape((BLOCK, D), F32),
        ),
        in_specs=[free] * 8 + [vmem] * ROWS,
        out_specs=(vmem,) * 5,
        scratch_shapes=[pltpu.SemaphoreType.DMA((8,))],
        compiler_params=params,
        name="prepare",
    )(*pieces, up2, up, own, down, down2)
    def attend(source, block):
        own = source == "own"
        part = shape((BLOCK, D), F32 if own else BF16)
        return pl.pallas_call(
            functools.partial(attend_kernel, source),
            out_shape=(shape((2 * H * NQ, D), F32), part) if own else part,
            in_specs=[smem] + [vmem] * (5 if own else 4),
            out_specs=(vmem, vmem) if own else vmem,
            scratch_shapes=[pltpu.VMEM((BLOCK, D), F32)],
            compiler_params=params,
            name="attend_" + source,
        )(lengths, block, w_all, keys, values, *((queries,) if own else ()))

    first = move_x(attend("first", first), -1)
    second = move_x(attend("second", second), 1)
    third = move_ctx(attend("third", third), 0, 2)
    ask, attended = attend("own", q)
    send = pl.pallas_call(
        finish_kernel,
        out_shape=shape((NC, PIECE, WIDE), BF16),
        in_specs=[vmem] * 9,
        out_specs=vmem,
        compiler_params=params,
        name="finish",
    )(up2, u, attended, first, second, third, w_out, w_all, ask)
    got = lax.all_to_all(send, "ctx", 0, 0, tiled=True)
    send = pl.pallas_call(
        turn_kernel,
        out_shape=shape((NC, PIECE, WIDE), BF16),
        in_specs=[smem, smem, vmem],
        out_specs=vmem,
        scratch_shapes=[pltpu.VMEM((USERS, 8, HD), F32)],
        compiler_params=params,
        name="turn",
    )(lengths, block_slots, got)
    got = lax.all_to_all(send, "ctx", 0, 0, tiled=True)
    return pl.pallas_call(
        last_kernel,
        out_shape=(shape((1, BLOCK, D), BF16), shape((1, USERS, NQ, D), F32)),
        in_specs=[vmem],
        out_specs=(vmem, vmem),
        compiler_params=params,
        name="last",
    )(got)


def solution(mesh):
    in_specs = (
        P("dp", "ctx", None),
        P("dp", None),
        P("dp", None),
        P(None, "dp"),
        P(),
        P(None, "dp"),
        P(),
    )
    out_specs = (P("dp", "ctx", None), P("dp", None, None, None))
    return jax.shard_map(shards, mesh=mesh, in_specs=in_specs, out_specs=out_specs, check_vma=False)
```

```python
import functools

import jax
import jax.numpy as jnp
from jax import lax
from jax.experimental import pallas as pl
from jax.experimental.pallas import tpu as pltpu
from jax.sharding import PartitionSpec as P

D = 512
H = 4
HD = 128
NQ = 8
BLOCK = 256
USERS = 4
NX = 4
NZ = 8
NC = NX * NZ
AHEAD = 2
SHIFT = AHEAD * NX
ROWS = 5
COLS = 256
POOL = 128
PIECE = BLOCK // NC
WIDE = D + HD
F32 = jnp.float32
BF16 = jnp.bfloat16
HALF_SCALE = 0.5 / (HD**0.5)


def normed(values):
    centered = values - jnp.mean(values, axis=-1, keepdims=True)
    spread = jnp.mean(centered * centered, axis=-1, keepdims=True)
    return centered * lax.rsqrt(spread + 1e-05)


def silu_of_twice(half):
    return half + half * jnp.tanh(half)


def project(rows, weight):
    return silu_of_twice(0.5 * jnp.dot(rows, weight, preferred_element_type=F32))


def place_in_user(lengths_ref, block):
    end = lengths_ref[0, 0]
    user = jnp.int32(0)
    start = jnp.int32(0)
    for other in range(USERS - 1):
        past = block >= end
        user = jnp.where(past, other + 1, user)
        start = jnp.where(past, end, start)
        end = end + lengths_ref[0, other + 1]
    return user, block - start


def my_place():
    place = lax.axis_index("ctx")
    lane = lax.axis_index("dp")
    return lax.div(place, NX), lax.rem(place, NX), lax.div(lane, 2), lax.rem(lane, 2)


def head(h):
    return slice(h * HD, (h + 1) * HD)


def prepare_kernel(*refs):
    shards_in, blocks = refs[:8], refs[8:13]
    w_ref, keys_ref, values_ref, sems = refs[13:]
    _, _, y, core = my_place()
    side = 1 - 2 * core

    def copy_in(ref, slot, part, columns):
        return pltpu.make_async_copy(
            ref.at[:, columns], w_ref.at[slot, :, columns], sems.at[part, slot]
        )

    main, pool = slice(0, COLS), slice(COLS, COLS + POOL)
    for part, columns in ((0, main), (1, pool)):
        for i, ref in enumerate(shards_in):
            there = core if i < 4 else 1 - core
            step = (0, -1, 1, 2)[i % 4]
            turn = side if i < 4 else -side
            slot = 2 * lax.rem(y + 4 + step * turn, 4) + there
            copy_in(ref, slot, part, columns).start()

    def wait(slot, part, columns):
        copy_in(shards_in[0], slot, part, columns).wait()

    rows = normed(blocks[0][...].astype(F32)).astype(BF16)
    for slot in (2, 3, 6, 7):
        wait(slot, 0, main)
    for j in range(ROWS):
        if j > 0:
            rows = normed(blocks[j][...].astype(F32)).astype(BF16)
        for half in range(2):
            part = slice(half * COLS, (half + 1) * COLS)
            values_ref[j, :, part] = project(rows, w_ref[2 + half, :, :COLS]).astype(BF16)
            keys_ref[j, :, part] = project(rows, w_ref[6 + half, :, :COLS]).astype(BF16)
    for slot in (0, 1, 4, 5):
        wait(slot, 0, main)
    for slot in range(8):
        wait(slot, 1, pool)


def attend_kernel(source, *refs):
    own = source == "own"
    lengths_ref, events_ref, w_ref, keys_ref, values_ref = refs[:5]
    out_ref, acc = refs[-2:]
    if own:
        ask_ref, ask_out_ref, u_ref = refs[5:8]
        for h in range(H):
            ask = lax.dot_general(
                ask_ref[:, head(h)],
                w_ref[h, :, COLS:],
                (((1,), (1,)), ((), ())),
                preferred_element_type=F32,
            )
            top = ask.astype(BF16).astype(F32)
            ask_out_ref[h * NQ : (h + 1) * NQ, :] = top
            ask_out_ref[(H + h) * NQ : (H + h + 1) * NQ, :] = ask - top
    z, x, _, core = my_place()
    turn = {"own": 0, "first": 3 - 2 * core, "second": 1 + 2 * core, "third": 2}[source]
    column = lax.rem(x + turn, NX)
    block = NX * lax.rem(z + AHEAD, NZ) + column
    _, before = place_in_user(lengths_ref, block)
    skip = jnp.where(column >= x, 0, 1)
    nearest = column - x + NX * skip
    count = jnp.where(before >= nearest, lax.div(before - nearest, NX) + 1, 0)

    rows = normed(events_ref[...].astype(F32)).astype(BF16)
    queries = [project(rows, w_ref[4 + half, :, :COLS]).astype(BF16) for half in range(2)]
    if own:
        for half in range(2):
            u_ref[:, half * COLS : (half + 1) * COLS] = project(rows, w_ref[half, :, :COLS])

    def weights_of(j, h, masked):
        scores = lax.dot_general(
            queries[h // 2][:, head(h % 2)],
            keys_ref[j, :, head(h)],
            (((1,), (1,)), ((), ())),
            preferred_element_type=F32,
        )
        weight = silu_of_twice(scores * HALF_SCALE)
        if masked:
            later = lax.broadcasted_iota(jnp.int32, (BLOCK, BLOCK), 1)
            weight = jnp.where(later <= lax.broadcasted_iota(jnp.int32, (BLOCK, BLOCK), 0), weight, 0.0)
        return weight.astype(BF16)

    def summed(weight, j, h):
        return jnp.dot(weight, values_ref[j, :, head(h)], preferred_element_type=F32)

    @pl.when(count == 4)
    def _():
        for h in range(H):
            weight = [weights_of(skip + j, h, own and j == 0) for j in range(4)]
            total = summed(weight[0], skip, h)
            for j in range(1, 4):
                total = total + summed(weight[j], skip + j, h)
            acc[:, head(h)] = total

    @pl.when(count < 4)
    def _():
        if own:
            weight = [weights_of(0, h, True) for h in range(H)]
            for h in range(H):
                acc[:, head(h)] = summed(weight[h], 0, h)
        else:
            acc[...] = jnp.zeros_like(acc)

        def step(j, carry):
            weight = [weights_of(skip + j, h, False) for h in range(H)]
            for h in range(H):
                acc[:, head(h)] += summed(weight[h], skip + j, h)
            return carry

        lax.fori_loop(1 if own else 0, count, step, 0)

    out_ref[...] = acc[...].astype(out_ref.dtype)


def finish_kernel(*refs):
    events_ref, u_ref = refs[:2]
    parts = refs[2:6]
    out_w_ref, w_ref, ask_ref, send_ref = refs[6:]
    attended = parts[0][...]
    for part in parts[1:]:
        attended = attended + part[...].astype(F32)
    mixed = (normed(attended) * u_ref[...]).astype(BF16)
    result = events_ref[...].astype(F32) + jnp.dot(
        mixed, out_w_ref[...], preferred_element_type=F32
    )
    result = result.astype(BF16)
    wide = result.astype(F32)
    for i in range(NC):
        send_ref[i, :, :D] = wide[i * PIECE : (i + 1) * PIECE].astype(BF16)
    scores = lax.dot_general(
        ask_ref[...].astype(BF16), result, (((1,), (1,)), ((), ())), preferred_element_type=F32
    )
    expo = jnp.exp((scores[: H * NQ] + scores[H * NQ :]) / (HD**0.5))
    top = expo.astype(BF16)
    both = jnp.concatenate([top, (expo - top.astype(F32)).astype(BF16)], axis=0)
    totals = jnp.broadcast_to(jnp.sum(expo, axis=1, keepdims=True), (H * NQ, HD))
    row = lax.broadcasted_iota(jnp.int32, (8, HD), 0)
    for h in range(H):
        value = jnp.dot(result, w_ref[H + h, :, COLS:], preferred_element_type=F32)
        value_top = value.astype(BF16)
        value_low = (value - value_top.astype(F32)).astype(BF16)
        mine = jnp.concatenate(
            [both[h * NQ : (h + 1) * NQ], both[(H + h) * NQ : (H + h + 1) * NQ]], axis=0
        )
        weighted = jnp.dot(mine, value_top, preferred_element_type=F32)
        weighted = weighted + jnp.dot(mine, value_low, preferred_element_type=F32)
        weighted = weighted[:NQ] + weighted[NQ:]
        total = totals[h * NQ : (h + 1) * NQ]
        weighted_top = weighted.astype(BF16).astype(F32)
        total_top = total.astype(BF16).astype(F32)
        for m in range(NQ):
            tile = jnp.where(row == 0, weighted_top[m : m + 1], 0.0)
            tile = jnp.where(row == 1, (weighted - weighted_top)[m : m + 1], tile)
            tile = jnp.where(row == 2, total_top[m : m + 1], tile)
            tile = jnp.where(row == 3, (total - total_top)[m : m + 1], tile)
            send_ref[m * H + h, :, D:] = tile.astype(BF16)


def turn_kernel(lengths_ref, slots_ref, got_ref, send_ref, sums):
    sums[...] = jnp.zeros_like(sums)
    for j in range(NC):
        user, _ = place_in_user(lengths_ref, jnp.int32((j + SHIFT) % NC))
        sums[user] += got_ref[j, :, D:].astype(F32)
    row = lax.broadcasted_iota(jnp.int32, (8, HD), 0)
    tile = jnp.zeros((8, HD), F32)
    for user in range(USERS):
        part = sums[user]
        mean = (part[0:1] + part[1:2]) / (part[2:3] + part[3:4])
        top = mean.astype(BF16).astype(F32)
        tile = jnp.where(row == user, top, tile)
        tile = jnp.where(row == user + USERS, mean - top, tile)
    tile = tile.astype(BF16)
    for s in range(NC):
        source = lax.rem(slots_ref[0, s] + (NC - SHIFT), NC)
        send_ref[s, :, :D] = got_ref[source, :, :D]
        send_ref[s, :, D:] = tile


def last_kernel(got_ref, out_ref, interests_ref):
    for i in range(0, NC, 2):
        pair = jnp.concatenate(
            [got_ref[i, :, :D].astype(F32), got_ref[i + 1, :, :D].astype(F32)], axis=0
        )
        out_ref[0, i * PIECE : (i + 2) * PIECE, :] = pair.astype(BF16)
    for m in range(NQ):
        for h in range(H):
            tile = got_ref[m * H + h, :, D:].astype(F32)
            mean = tile[:USERS] + tile[USERS:]
            for user in range(USERS):
                interests_ref[0, user, m : m + 1, h * HD : (h + 1) * HD] = mean[user : user + 1]


def move_ctx(values, dz, dx):
    pairs = []
    for z in range(NZ):
        for x in range(NX):
            pairs.append((z * NX + x, ((z + dz) % NZ) * NX + (x + dx) % NX))
    return lax.ppermute(values, "ctx", pairs)


def move_x(values, dx):
    pairs = []
    for lane in range(8):
        for z in range(NZ):
            for x in range(NX):
                there = (x + (dx if lane % 2 == 0 else -dx)) % NX
                pairs.append((lane * NC + z * NX + x, lane * NC + z * NX + there))
    return lax.ppermute(values, ("dp", "ctx"), pairs)


def move_y(values, dy):
    pairs = []
    for y in range(4):
        for core in range(2):
            there = (y + (dy if core == 0 else -dy)) % 4
            pairs.append((2 * y + core, 2 * there + core))
    return lax.ppermute(values, "dp", pairs)


def swap_cores(values):
    return lax.ppermute(values, "dp", [(lane, lane ^ 1) for lane in range(8)])


def shards(events, lengths, block_slots, w_in, w_out, w_pool, queries):
    own = events[0]
    smem = pl.BlockSpec(memory_space=pltpu.SMEM)
    vmem = pl.BlockSpec(memory_space=pltpu.VMEM)
    free = pl.BlockSpec(memory_space=pl.ANY)
    params = pltpu.CompilerParams(vmem_limit_bytes=16 * 1024 * 1024)
    shape = jax.ShapeDtypeStruct
    some = lengths[0, 0] > 0
    up = move_ctx(own, -1, 0)
    down = move_ctx(own, 1, 0)
    up2 = move_ctx(jnp.where(some, up, down), -1, 0)
    down2 = move_ctx(down, 1, 0)
    asked = up2
    weights = lax.pad(w_in, jnp.bfloat16(0), ((0, 0, 0), (0, POOL, 0))) + lax.pad(
        w_pool, jnp.bfloat16(0), ((0, 0, 0), (COLS, 0, 0))
    )
    weights_a = move_y(weights, 1)
    weights_b = move_y(weights, -1)
    first = move_x(asked, 1)
    second = move_x(asked, -1)
    third = move_ctx(asked, 0, 2)
    weights_c = move_y(weights_a, 1)
    mine = [weights, weights_a, weights_b, weights_c]
    pieces = mine + [swap_cores(one) for one in mine]
    w_all, keys, values = pl.pallas_call(
        prepare_kernel,
        out_shape=(
            shape((8, D, COLS + POOL), BF16),
            shape((ROWS, BLOCK, D), BF16),
            shape((ROWS, BLOCK, D), BF16),
        ),
        in_specs=[free] * 8 + [vmem] * ROWS,
        out_specs=(vmem,) * 3,
        scratch_shapes=[pltpu.SemaphoreType.DMA((2, 8))],
        compiler_params=params,
        name="prepare",
    )(*pieces, up2, up, own, down, down2)
    def attend(source, block):
        own = source == "own"
        part = shape((BLOCK, D), F32 if own else BF16)
        return pl.pallas_call(
            functools.partial(attend_kernel, source),
            out_shape=(shape((2 * H * NQ, D), F32), shape((BLOCK, D), F32), part) if own else part,
            in_specs=[smem] + [vmem] * (5 if own else 4),
            out_specs=(vmem,) * 3 if own else vmem,
            scratch_shapes=[pltpu.VMEM((BLOCK, D), F32)],
            compiler_params=params,
            name="attend_" + source,
        )(lengths, block, w_all, keys, values, *((queries,) if own else ()))

    first = move_x(attend("first", first), -1)
    second = move_x(attend("second", second), 1)
    third = move_ctx(attend("third", third), 0, 2)
    ask, u, attended = attend("own", up2)
    send = pl.pallas_call(
        finish_kernel,
        out_shape=shape((NC, PIECE, WIDE), BF16),
        in_specs=[vmem] * 9,
        out_specs=vmem,
        compiler_params=params,
        name="finish",
    )(up2, u, attended, first, second, third, w_out, w_all, ask)
    got = lax.all_to_all(send, "ctx", 0, 0, tiled=True)
    send = pl.pallas_call(
        turn_kernel,
        out_shape=shape((NC, PIECE, WIDE), BF16),
        in_specs=[smem, smem, vmem],
        out_specs=vmem,
        scratch_shapes=[pltpu.VMEM((USERS, 8, HD), F32)],
        compiler_params=params,
        name="turn",
    )(lengths, block_slots, got)
    got = lax.all_to_all(send, "ctx", 0, 0, tiled=True)
    return pl.pallas_call(
        last_kernel,
        out_shape=(shape((1, BLOCK, D), BF16), shape((1, USERS, NQ, D), F32)),
        in_specs=[vmem],
        out_specs=(vmem, vmem),
        compiler_params=params,
        name="last",
    )(got)


def solution(mesh):
    in_specs = (
        P("dp", "ctx", None),
        P("dp", None),
        P("dp", None),
        P(None, "dp"),
        P(),
        P(None, "dp"),
        P(),
    )
    out_specs = (P("dp", "ctx", None), P("dp", None, None, None))
    return jax.shard_map(shards, mesh=mesh, in_specs=in_specs, out_specs=out_specs, check_vma=False)
```

```python
import functools

import jax
import jax.numpy as jnp
from jax import lax
from jax.experimental import pallas as pl
from jax.experimental.pallas import tpu as pltpu
from jax.sharding import PartitionSpec as P

D = 512
H = 4
HD = 128
NQ = 8
BLOCK = 256
USERS = 4
NX = 4
NZ = 8
NC = NX * NZ
AHEAD = 2
SHIFT = AHEAD * NX
ROWS = 5
COLS = 256
POOL = 128
PIECE = BLOCK // NC
WIDE = D + HD
F32 = jnp.float32
BF16 = jnp.bfloat16
HALF_SCALE = 0.5 / (HD**0.5)


def normed(values):
    centered = values - jnp.mean(values, axis=-1, keepdims=True)
    spread = jnp.mean(centered * centered, axis=-1, keepdims=True)
    return centered * lax.rsqrt(spread + 1e-05)


def silu_of_twice(half):
    return half + half * jnp.tanh(half)


def project(rows, weight):
    return silu_of_twice(0.5 * jnp.dot(rows, weight, preferred_element_type=F32))


def place_in_user(lengths_ref, block):
    end = lengths_ref[0, 0]
    user = jnp.int32(0)
    start = jnp.int32(0)
    for other in range(USERS - 1):
        past = block >= end
        user = jnp.where(past, other + 1, user)
        start = jnp.where(past, end, start)
        end = end + lengths_ref[0, other + 1]
    return user, block - start


def my_place():
    place = lax.axis_index("ctx")
    lane = lax.axis_index("dp")
    return lax.div(place, NX), lax.rem(place, NX), lax.div(lane, 2), lax.rem(lane, 2)


def head(h):
    return slice(h * HD, (h + 1) * HD)


def prepare_kernel(*refs):
    shards_in, blocks = refs[:8], refs[8:13]
    w_ref, keys_ref, values_ref, sems = refs[13:]
    _, _, y, core = my_place()
    side = 1 - 2 * core

    def copy_in(ref, slot, part, columns):
        return pltpu.make_async_copy(
            ref.at[:, columns], w_ref.at[slot, :, columns], sems.at[part, slot]
        )

    main, pool = slice(0, COLS), slice(COLS, COLS + POOL)
    for part, columns in ((0, main), (1, pool)):
        for i, ref in enumerate(shards_in):
            there = core if i < 4 else 1 - core
            step = (0, -1, 1, 2)[i % 4]
            turn = side if i < 4 else -side
            slot = 2 * lax.rem(y + 4 + step * turn, 4) + there
            copy_in(ref, slot, part, columns).start()

    def wait(slot, part, columns):
        copy_in(shards_in[0], slot, part, columns).wait()

    rows = normed(blocks[0][...].astype(F32)).astype(BF16)
    for slot in (2, 3, 6, 7):
        wait(slot, 0, main)
    for j in range(ROWS):
        if j > 0:
            rows = normed(blocks[j][...].astype(F32)).astype(BF16)
        for half in range(2):
            part = slice(half * COLS, (half + 1) * COLS)
            values_ref[j, :, part] = project(rows, w_ref[2 + half, :, :COLS]).astype(BF16)
            keys_ref[j, :, part] = project(rows, w_ref[6 + half, :, :COLS]).astype(BF16)
    for slot in (0, 1, 4, 5):
        wait(slot, 0, main)
    for slot in range(8):
        wait(slot, 1, pool)


def attend_kernel(source, *refs):
    own = source == "own"
    lengths_ref, events_ref, w_ref, keys_ref, values_ref = refs[:5]
    out_ref, acc = refs[-2:]
    if own:
        ask_ref, ask_out_ref, u_ref = refs[5:8]
        for h in range(H):
            ask = lax.dot_general(
                ask_ref[:, head(h)],
                w_ref[h, :, COLS:],
                (((1,), (1,)), ((), ())),
                preferred_element_type=F32,
            )
            top = ask.astype(BF16).astype(F32)
            ask_out_ref[h * NQ : (h + 1) * NQ, :] = top
            ask_out_ref[(H + h) * NQ : (H + h + 1) * NQ, :] = ask - top
    z, x, _, core = my_place()
    turn = {"own": 0, "first": 3 - 2 * core, "second": 1 + 2 * core, "third": 2}[source]
    column = lax.rem(x + turn, NX)
    block = NX * lax.rem(z + AHEAD, NZ) + column
    _, before = place_in_user(lengths_ref, block)
    skip = jnp.where(column >= x, 0, 1)
    nearest = column - x + NX * skip
    count = jnp.where(before >= nearest, lax.div(before - nearest, NX) + 1, 0)

    rows = normed(events_ref[...].astype(F32)).astype(BF16)
    queries = [project(rows, w_ref[4 + half, :, :COLS]).astype(BF16) for half in range(2)]
    if own:
        for half in range(2):
            u_ref[:, half * COLS : (half + 1) * COLS] = project(rows, w_ref[half, :, :COLS])

    def weights_of(j, h, masked):
        scores = lax.dot_general(
            queries[h // 2][:, head(h % 2)],
            keys_ref[j, :, head(h)],
            (((1,), (1,)), ((), ())),
            preferred_element_type=F32,
        )
        weight = silu_of_twice(scores * HALF_SCALE)
        if masked:
            later = lax.broadcasted_iota(jnp.int32, (BLOCK, BLOCK), 1)
            weight = jnp.where(later <= lax.broadcasted_iota(jnp.int32, (BLOCK, BLOCK), 0), weight, 0.0)
        return weight.astype(BF16)

    def summed(weight, j, h):
        return jnp.dot(weight, values_ref[j, :, head(h)], preferred_element_type=F32)

    @pl.when(count == 4)
    def _():
        for h in range(H):
            weight = [weights_of(skip + j, h, own and j == 0) for j in range(4)]
            total = summed(weight[0], skip, h)
            for j in range(1, 4):
                total = total + summed(weight[j], skip + j, h)
            acc[:, head(h)] = total

    @pl.when(count < 4)
    def _():
        if own:
            weight = [weights_of(0, h, True) for h in range(H)]
            for h in range(H):
                acc[:, head(h)] = summed(weight[h], 0, h)
        else:
            acc[...] = jnp.zeros_like(acc)

        def step(j, carry):
            weight = [weights_of(skip + j, h, False) for h in range(H)]
            for h in range(H):
                acc[:, head(h)] += summed(weight[h], skip + j, h)
            return carry

        lax.fori_loop(1 if own else 0, count, step, 0)

    out_ref[...] = acc[...].astype(out_ref.dtype)


def finish_kernel(*refs):
    events_ref, u_ref = refs[:2]
    parts = refs[2:6]
    out_w_ref, w_ref, ask_ref, send_ref = refs[6:]
    attended = parts[0][...]
    for part in parts[1:]:
        attended = attended + part[...].astype(F32)
    mixed = (normed(attended) * u_ref[...]).astype(BF16)
    result = events_ref[...].astype(F32) + jnp.dot(
        mixed, out_w_ref[...], preferred_element_type=F32
    )
    result = result.astype(BF16)
    wide = result.astype(F32)
    for i in range(NC):
        send_ref[i, :, :D] = wide[i * PIECE : (i + 1) * PIECE].astype(BF16)
    scores = lax.dot_general(
        ask_ref[...].astype(BF16), result, (((1,), (1,)), ((), ())), preferred_element_type=F32
    )
    expo = jnp.exp((scores[: H * NQ] + scores[H * NQ :]) / (HD**0.5))
    top = expo.astype(BF16)
    both = jnp.concatenate([top, (expo - top.astype(F32)).astype(BF16)], axis=0)
    totals = jnp.broadcast_to(jnp.sum(expo, axis=1, keepdims=True), (H * NQ, HD))
    row = lax.broadcasted_iota(jnp.int32, (8, HD), 0)
    for h in range(H):
        value = jnp.dot(result, w_ref[H + h, :, COLS:], preferred_element_type=F32)
        value_top = value.astype(BF16)
        value_low = (value - value_top.astype(F32)).astype(BF16)
        mine = jnp.concatenate(
            [both[h * NQ : (h + 1) * NQ], both[(H + h) * NQ : (H + h + 1) * NQ]], axis=0
        )
        weighted = jnp.dot(mine, value_top, preferred_element_type=F32)
        weighted = weighted + jnp.dot(mine, value_low, preferred_element_type=F32)
        weighted = weighted[:NQ] + weighted[NQ:]
        total = totals[h * NQ : (h + 1) * NQ]
        weighted_top = weighted.astype(BF16).astype(F32)
        total_top = total.astype(BF16).astype(F32)
        for m in range(NQ):
            tile = jnp.where(row == 0, weighted_top[m : m + 1], 0.0)
            tile = jnp.where(row == 1, (weighted - weighted_top)[m : m + 1], tile)
            tile = jnp.where(row == 2, total_top[m : m + 1], tile)
            tile = jnp.where(row == 3, (total - total_top)[m : m + 1], tile)
            send_ref[m * H + h, :, D:] = tile.astype(BF16)


def turn_kernel(lengths_ref, slots_ref, got_ref, send_ref, sums):
    sums[...] = jnp.zeros_like(sums)
    for j in range(NC):
        user, _ = place_in_user(lengths_ref, jnp.int32((j + SHIFT) % NC))
        sums[user] += got_ref[j, :, D:].astype(F32)
    row = lax.broadcasted_iota(jnp.int32, (8, HD), 0)
    tile = jnp.zeros((8, HD), F32)
    for user in range(USERS):
        part = sums[user]
        mean = (part[0:1] + part[1:2]) / (part[2:3] + part[3:4])
        top = mean.astype(BF16).astype(F32)
        tile = jnp.where(row == user, top, tile)
        tile = jnp.where(row == user + USERS, mean - top, tile)
    tile = tile.astype(BF16)
    for s in range(NC):
        source = lax.rem(slots_ref[0, s] + (NC - SHIFT), NC)
        send_ref[s, :, :D] = got_ref[source, :, :D]
        send_ref[s, :, D:] = tile


def last_kernel(got_ref, out_ref, interests_ref):
    for i in range(0, NC, 2):
        pair = jnp.concatenate(
            [got_ref[i, :, :D].astype(F32), got_ref[i + 1, :, :D].astype(F32)], axis=0
        )
        out_ref[0, i * PIECE : (i + 2) * PIECE, :] = pair.astype(BF16)
    for m in range(NQ):
        for h in range(H):
            tile = got_ref[m * H + h, :, D:].astype(F32)
            mean = tile[:USERS] + tile[USERS:]
            for user in range(USERS):
                interests_ref[0, user, m : m + 1, h * HD : (h + 1) * HD] = mean[user : user + 1]


def move_ctx(values, dz, dx):
    pairs = []
    for z in range(NZ):
        for x in range(NX):
            pairs.append((z * NX + x, ((z + dz) % NZ) * NX + (x + dx) % NX))
    return lax.ppermute(values, "ctx", pairs)


def move_x(values, dx):
    pairs = []
    for lane in range(8):
        for z in range(NZ):
            for x in range(NX):
                there = (x + (dx if lane % 2 == 0 else -dx)) % NX
                pairs.append((lane * NC + z * NX + x, lane * NC + z * NX + there))
    return lax.ppermute(values, ("dp", "ctx"), pairs)


def move_y(values, dy):
    pairs = []
    for y in range(4):
        for core in range(2):
            there = (y + (dy if core == 0 else -dy)) % 4
            pairs.append((2 * y + core, 2 * there + core))
    return lax.ppermute(values, "dp", pairs)


def swap_cores(values):
    return lax.ppermute(values, "dp", [(lane, lane ^ 1) for lane in range(8)])


def shards(events, lengths, block_slots, w_in, w_out, w_pool, queries):
    own = events[0]
    smem = pl.BlockSpec(memory_space=pltpu.SMEM)
    vmem = pl.BlockSpec(memory_space=pltpu.VMEM)
    free = pl.BlockSpec(memory_space=pl.ANY)
    params = pltpu.CompilerParams(vmem_limit_bytes=16 * 1024 * 1024)
    shape = jax.ShapeDtypeStruct
    some = lengths[0, 0] > 0
    up = move_ctx(own, -1, 0)
    down = move_ctx(own, 1, 0)
    up2 = move_ctx(up, -1, 0)
    down2 = move_ctx(jnp.where(some, down, up), 1, 0)
    asked = up2
    weights = lax.pad(w_in, jnp.bfloat16(0), ((0, 0, 0), (0, POOL, 0))) + lax.pad(
        w_pool, jnp.bfloat16(0), ((0, 0, 0), (COLS, 0, 0))
    )
    weights_a = move_y(weights, 1)
    weights_b = move_y(weights, -1)
    first = move_x(asked, 1)
    second = move_x(asked, -1)
    third = move_ctx(asked, 0, 2)
    weights_c = move_y(weights_a, 1)
    mine = [weights, weights_a, weights_b, weights_c]
    pieces = mine + [swap_cores(one) for one in mine]
    w_all, keys, values = pl.pallas_call(
        prepare_kernel,
        out_shape=(
            shape((8, D, COLS + POOL), BF16),
            shape((ROWS, BLOCK, D), BF16),
            shape((ROWS, BLOCK, D), BF16),
        ),
        in_specs=[free] * 8 + [vmem] * ROWS,
        out_specs=(vmem,) * 3,
        scratch_shapes=[pltpu.SemaphoreType.DMA((2, 8))],
        compiler_params=params,
        name="prepare",
    )(*pieces, up2, up, own, down, down2)
    def attend(source, block):
        own = source == "own"
        part = shape((BLOCK, D), F32 if own else BF16)
        return pl.pallas_call(
            functools.partial(attend_kernel, source),
            out_shape=(shape((2 * H * NQ, D), F32), shape((BLOCK, D), F32), part) if own else part,
            in_specs=[smem] + [vmem] * (5 if own else 4),
            out_specs=(vmem,) * 3 if own else vmem,
            scratch_shapes=[pltpu.VMEM((BLOCK, D), F32)],
            compiler_params=params,
            name="attend_" + source,
        )(lengths, block, w_all, keys, values, *((queries,) if own else ()))

    first = move_x(attend("first", first), -1)
    second = move_x(attend("second", second), 1)
    third = move_ctx(attend("third", third), 0, 2)
    ask, u, attended = attend("own", up2)
    send = pl.pallas_call(
        finish_kernel,
        out_shape=shape((NC, PIECE, WIDE), BF16),
        in_specs=[vmem] * 9,
        out_specs=vmem,
        compiler_params=params,
        name="finish",
    )(up2, u, attended, first, second, third, w_out, w_all, ask)
    got = lax.all_to_all(send, "ctx", 0, 0, tiled=True)
    send = pl.pallas_call(
        turn_kernel,
        out_shape=shape((NC, PIECE, WIDE), BF16),
        in_specs=[smem, smem, vmem],
        out_specs=vmem,
        scratch_shapes=[pltpu.VMEM((USERS, 8, HD), F32)],
        compiler_params=params,
        name="turn",
    )(lengths, block_slots, got)
    got = lax.all_to_all(send, "ctx", 0, 0, tiled=True)
    return pl.pallas_call(
        last_kernel,
        out_shape=(shape((1, BLOCK, D), BF16), shape((1, USERS, NQ, D), F32)),
        in_specs=[vmem],
        out_specs=(vmem, vmem),
        compiler_params=params,
        name="last",
    )(got)


def solution(mesh):
    in_specs = (
        P("dp", "ctx", None),
        P("dp", None),
        P("dp", None),
        P(None, "dp"),
        P(),
        P(None, "dp"),
        P(),
    )
    out_specs = (P("dp", "ctx", None), P("dp", None, None, None))
    return jax.shard_map(shards, mesh=mesh, in_specs=in_specs, out_specs=out_specs, check_vma=False)
```
